32 devices in a mesh: blk: 16 (over z, y, core), par: 2 (over x).
Axes of the slice: x: 2, y: 2, z: 4, core: 2. Of those that a mesh axis runs over, the one named last changes fastest.
Arguments:
- logder: float32 [2048, 6144], P('blk', 'par'), may hold values from -50 to 50
Outputs:
- kernel_tiles: float32 [16, 9, 128, 128], P('blk', None, 'par')
The draws below stay inside these ranges and needn't reach their ends.
All inputs are finite; a program needn't handle non-finite values.
Results may differ from the reference program's by a relative error of at most 0.00015.
Values sent between devices are 32-bit elements; how exact they have to be, the bound alone decides.
No kernel may reach another device: no remote copies, remote signals or barrier semaphores. Data moves between devices by JAX's collectives and lax.ppermute only.
A program may use at most 64 MiB of HBM per device.

```python
import math
import jax
import jax.numpy as jnp
from jax import lax

BS = 128
P_SIZE = 6144
NS = 2048
TILES = 9
N_BLK = 16


def draw_logder(key, part):
    keys = jax.random.split(jax.random.fold_in(key, 7), 4)
    row_scale = jnp.exp(jax.random.uniform(keys[0], (NS, 1), jnp.float32, math.log(0.3), math.log(3.0)))
    col_scale = jnp.exp(jax.random.uniform(keys[1], (1, P_SIZE), jnp.float32, math.log(0.5), math.log(2.0)))
    offset = 1.5 * jax.random.truncated_normal(keys[3], -4.0, 4.0, (1, P_SIZE), jnp.float32)
    ramp = 1.0 + 2.0 * jnp.arange(NS, dtype=jnp.float32)[:, None] / NS
    noise = jax.random.truncated_normal(keys[2], -5.0, 5.0, (NS, P_SIZE), jnp.float32)
    return row_scale * col_scale * noise + offset * ramp


def setup_inputs(seed: int = 0) -> dict:
    seeds = jax.random.split(jax.random.key(seed), 2)
    return {
        "logder": draw_logder(jax.random.fold_in(seeds[1], 71), 0),
    }


def reference(logder):
    mean = jnp.sum(logder, axis=0) / NS
    centered = logder - mean[None, :]
    blocks = centered.reshape(N_BLK, BS, P_SIZE)

    def one_block(index):
        rows = lax.dynamic_index_in_dim(blocks, index, 0, keepdims=False)
        columns = jnp.roll(blocks, -index, axis=0)[:TILES]
        return jnp.einsum("rp,dcp->drc", rows, columns, precision=lax.Precision.HIGHEST) / P_SIZE

    return lax.map(one_block, jnp.arange(N_BLK, dtype=jnp.int32))
```

```python
import jax
import jax.numpy as jnp
from jax import lax
from jax.sharding import PartitionSpec as P


def swap(value, axis, mask):
    return lax.ppermute(value, axis, [(k, k ^ mask) for k in range(lax.axis_size(axis))])


def pick(value, index, axis):
    return lax.dynamic_index_in_dim(value, index, axis, keepdims=False)


def on_device(logder):
    nblocks = lax.axis_size("blk")
    nshards = lax.axis_size("par")
    rows, width = logder.shape
    me = lax.axis_index("blk")
    levels = 2
    group = 1 << levels
    planes = nblocks // group
    tiles = nblocks // 2 + 1
    factor = 1.0 / (width * nshards)

    sums = lax.all_gather(jnp.sum(logder, axis=0), "blk")

    piece = logder[None]
    offset = 0
    for level in range(levels):
        bit = (me >> level) & 1
        part = piece.shape[-1] // 2
        mine = lax.dynamic_slice_in_dim(piece, bit * part, part, 2)
        other = lax.dynamic_slice_in_dim(piece, (1 - bit) * part, part, 2)
        offset = offset + bit * part
        got = swap(other, "blk", 1 << level)
        piece = jnp.where(
            bit == 0, jnp.concatenate([mine, got]), jnp.concatenate([got, mine])
        )
    part = piece.shape[-1]
    slab = piece.reshape(group * rows, part)
    mean = jnp.sum(lax.dynamic_slice_in_dim(sums, offset, part, 1), axis=0) / (rows * nblocks)

    left = slab - mean
    down = [(k, (k - group) % nblocks) for k in range(nblocks)]
    current = slab
    products = []
    for step in range(planes // 2 + 1):
        products.append(
            lax.dot_general(
                left,
                current - mean,
                (((1,), (1,)), ((), ())),
                precision=lax.Precision.HIGH,
                preferred_element_type=jnp.float32,
            )
        )
        if step < planes // 2:
            current = lax.ppermute(current, "blk", down)
    full = jnp.concatenate(products, axis=1)
    full = full.reshape(group, rows, -1)
    share = jnp.stack(
        [full[k, :, k * rows : (k + tiles) * rows] for k in range(group)]
    )
    for level in range(levels):
        bit = (me >> level) & 1
        share = share.reshape(share.shape[0] // 2, 2, rows, tiles * rows)
        got = swap(pick(share, 1 - bit, 1), "blk", 1 << level)
        share = pick(share, bit, 1) + got
    share = share[0]
    shard = lax.axis_index("par")
    mask = nshards // 2
    while mask:
        bit = (shard // mask) % 2
        share = share.reshape(2, share.shape[-2] // 2, tiles * rows)
        got = swap(pick(share, 1 - bit, 0), "par", mask)
        share = pick(share, bit, 0) + got
        mask //= 2
    out = (share * factor).reshape(rows // nshards, tiles, rows)
    return jnp.swapaxes(out, 0, 1)[None]


def solution(mesh):
    placed = (P("blk", "par"),)
    return jax.shard_map(
        on_device,
        mesh=mesh,
        in_specs=placed,
        out_specs=P("blk", None, "par", None),
        check_vma=False,
    )
```

```python
import functools
import jax
import jax.numpy as jnp
from jax import lax
from jax.experimental import pallas as pl
from jax.experimental.pallas import tpu as pltpu
from jax.sharding import PartitionSpec as P


def swap(value, mask):
    return lax.ppermute(value, "blk", [(k, k ^ mask) for k in range(lax.axis_size("blk"))])


def pick(value, index, axis=0):
    return lax.dynamic_index_in_dim(value, index, axis, keepdims=False)


def hop(value, mask, turn):
    shards = lax.axis_size("par")
    pairs = [
        (k * shards + s, (k ^ mask) * shards + (s + turn) % shards)
        for k in range(lax.axis_size("blk"))
        for s in range(shards)
    ]
    return lax.ppermute(value, ("blk", "par"), pairs)


def split(value):
    high = value.astype(jnp.bfloat16)
    return high, (value - high.astype(jnp.float32)).astype(jnp.bfloat16)


def product(left, right):
    def dot(a, b):
        return lax.dot_general(
            a, b, (((1,), (1,)), ((), ())), preferred_element_type=jnp.float32
        )

    return dot(left[0], right[0]) + (dot(left[0], right[1]) + dot(left[1], right[0]))


def pair_kernel(near_l, far_l, near_r, far_r, mean_ref, keep_ref, send_ref):
    mean = mean_ref[...]
    rows = near_l.shape[1]
    shards, part = keep_ref.shape[1], keep_ref.shape[3]

    def centered(ref):
        value = ref[...]
        return split(value.reshape(2 * rows, value.shape[2]) - mean)

    rights = [centered(near_r), centered(far_r)]
    for a, ref in enumerate((near_l, far_l)):
        left = centered(ref)
        for b, right in enumerate(rights):
            block = product(left, right)
            for core, out in enumerate((keep_ref, send_ref)):
                for other in range(2):
                    place = (2 * b + other) ^ (2 * a + core)
                    tile = block[core * rows : (core + 1) * rows, other * rows : (other + 1) * rows]
                    for s in range(shards):
                        out[a, s, place] = tile[s * part : (s + 1) * part]


def pair(left, right, mean, shards):
    _, rows, width = left[0].shape
    shape = jax.ShapeDtypeStruct((2, shards, 4, rows // shards, rows), jnp.float32)
    return pl.pallas_call(
        pair_kernel,
        out_shape=(shape, shape),
        compiler_params=pltpu.CompilerParams(vmem_limit_bytes=40 << 20),
        cost_estimate=pl.CostEstimate(
            flops=6 * 16 * rows * rows * width,
            bytes_accessed=4 * (8 * rows * width + 16 * rows * rows),
            transcendentals=0,
        ),
    )(*left, *right, mean)


def gather_share(keep, send, shard):
    shards = keep.shape[1]
    total = keep + swap(send, 1)
    near, far = total[0], total[1]
    result = pick(near, shard)
    for turn in range(shards):
        to = (shard + turn) % shards
        result = result + hop(pick(far, to), 2, turn)
        if turn:
            result = result + hop(pick(near, to), 0, turn)
    return result


def final_kernel(factor, where_ref, share_ref, out_ref):
    for d in range(out_ref.shape[0]):
        out_ref[d] = share_ref[where_ref[d]] * factor


def on_device(logder):
    nblocks = lax.axis_size("blk")
    nshards = lax.axis_size("par")
    rows, width = logder.shape
    me = lax.axis_index("blk")
    shard = lax.axis_index("par")
    planes = nblocks // 4
    tiles = nblocks // 2 + 1
    factor = 1.0 / (width * nshards)
    half, quarter = width // 2, width // 4
    core, side = me & 1, (me >> 1) & 1

    theirs = swap(lax.dynamic_slice_in_dim(logder, (1 - core) * half, half, 1), 1)

    def both(which):
        mine = lax.dynamic_slice_in_dim(logder, core * half + which * quarter, quarter, 1)
        return jnp.stack([mine, lax.dynamic_slice_in_dim(theirs, which * quarter, quarter, 1)])

    near, away = both(side), both(1 - side)
    far = swap(away, 2)
    sums = jnp.sum(near, axis=(0, 1))[None]
    sums = sums + swap(jnp.sum(away, axis=(0, 1))[None], 2)
    mask = 4
    while mask < nblocks:
        sums = sums + swap(sums, mask)
        mask *= 2
    mean = sums / (rows * nblocks)

    down = [(k, (k - 4) % nblocks) for k in range(nblocks)]
    left = (near, far)
    right = left
    shares = []
    for step in range(planes // 2 + 1):
        keep, send = pair(left, right, mean, nshards)
        shares.append(gather_share(keep, send, shard))
        if step < planes // 2:
            right = tuple(lax.ppermute(value, "blk", down) for value in right)
    share = jnp.concatenate(shares, axis=0)

    place = me % 4
    position = place + jnp.arange(tiles, dtype=jnp.int32)
    where = position - position % 4 + ((position % 4) ^ place)
    out = pl.pallas_call(
        functools.partial(final_kernel, factor),
        out_shape=jax.ShapeDtypeStruct((tiles, rows // nshards, rows), jnp.float32),
        in_specs=[
            pl.BlockSpec(memory_space=pltpu.SMEM),
            pl.BlockSpec(memory_space=pltpu.VMEM),
        ],
    )(where, share)
    return out[None]


def solution(mesh):
    placed = (P("blk", "par"),)
    return jax.shard_map(
        on_device,
        mesh=mesh,
        in_specs=placed,
        out_specs=P("blk", None, "par", None),
        check_vma=False,
    )
```

```python
import functools
import jax
import jax.numpy as jnp
from jax import lax
from jax.experimental import pallas as pl
from jax.experimental.pallas import tpu as pltpu
from jax.sharding import PartitionSpec as P


def swap(value, mask):
    return lax.ppermute(value, "blk", [(k, k ^ mask) for k in range(lax.axis_size("blk"))])


def shift(value, steps):
    count = lax.axis_size("blk")
    return lax.ppermute(value, "blk", [(k, (k + steps) % count) for k in range(count)])


def hop(value, mask, turn):
    shards = lax.axis_size("par")
    pairs = [
        (k * shards + s, (k ^ mask) * shards + (s + turn) % shards)
        for k in range(lax.axis_size("blk"))
        for s in range(shards)
    ]
    return lax.ppermute(value, ("blk", "par"), pairs)


def pick(value, index, axis=0):
    return lax.dynamic_index_in_dim(value, index, axis, keepdims=False)


def split(value):
    high = value.astype(jnp.bfloat16)
    return high, (value - high.astype(jnp.float32)).astype(jnp.bfloat16)


def product(left, right):
    def dot(a, b):
        return lax.dot_general(
            a, b, (((1,), (1,)), ((), ())), preferred_element_type=jnp.float32
        )

    return dot(left[0], right[0]) + (dot(left[0], right[1]) + dot(left[1], right[0]))


def store(block, out_refs, a, b, first):
    keep_ref = out_refs[0]
    shards, part, rows = keep_ref.shape[1], keep_ref.shape[3], keep_ref.shape[4]
    for core, out in enumerate(out_refs):
        for other in range(2):
            place = first + ((2 * b + other) ^ (2 * a + core))
            tile = block[core * rows : (core + 1) * rows, other * rows : (other + 1) * rows]
            for s in range(shards):
                out[a, s, place] = tile[s * part : (s + 1) * part]


def centered(ref, mean):
    value = ref[...]
    return split(value.reshape(value.shape[0] * value.shape[1], value.shape[2]) - mean)


def own_kernel(near0, far0, near1, far1, mean_ref, keep_ref, send_ref, high_ref, low_ref):
    sides = []
    for chunk, refs in enumerate(((near0, far0), (near1, far1))):
        for a, ref in enumerate(refs):
            high, low = centered(ref, mean_ref[chunk])
            high_ref[chunk, a], low_ref[chunk, a] = high, low
            sides.append((high, low))
    for a in range(2):
        for b in range(2):
            block = product(sides[a], sides[b]) + product(sides[2 + a], sides[2 + b])
            store(block, (keep_ref, send_ref), a, b, 0)


def pair_kernel(columns, flag_ref, mean_ref, high_ref, low_ref, *refs):
    out_refs = refs[-2:]
    flag = flag_ref[0]
    if len(refs) > 2 * len(columns) + 2:
        for old, new in zip(refs[-4:-2], out_refs):
            for a in range(2):
                for place in range(4):
                    if (place ^ (2 * a)) // 2 not in columns:
                        new[a, :, place] = old[a, :, place]
    for position, b in enumerate(columns):
        rights = [
            centered(refs[2 * position + chunk], mean_ref[chunk ^ flag]) for chunk in range(2)
        ]
        for a in range(2):
            block = None
            for chunk in range(2):
                at = chunk ^ flag
                term = product((high_ref[at, a], low_ref[at, a]), rights[chunk])
                block = term if block is None else block + term
            store(block, out_refs, a, b, 0)


def half_kernel(mean_ref, high_ref, low_ref, near_ref, far_ref, keep_ref, send_ref):
    lefts = [(high_ref[1, a], low_ref[1, a]) for a in range(2)]
    rights = [centered(ref, mean_ref[1]) for ref in (near_ref, far_ref)]
    for a in range(2):
        for b in range(2):
            store(product(lefts[a], rights[b]), (keep_ref, send_ref), a, b, 0)
            store(product(rights[a], lefts[b]), (keep_ref, send_ref), a, b, 4)


VMEM = pl.BlockSpec(memory_space=pltpu.VMEM)
SMEM = pl.BlockSpec(memory_space=pltpu.SMEM)


def call(kernel, outs, scalars, arrays, flops):
    moved = sum(4 * v.size for v in arrays) + sum(4 * v.size for v in outs)
    return pl.pallas_call(
        kernel,
        out_shape=outs,
        in_specs=[SMEM] * len(scalars) + [VMEM] * len(arrays),
        out_specs=(VMEM,) * len(outs),
        compiler_params=pltpu.CompilerParams(vmem_limit_bytes=16 << 20),
        cost_estimate=pl.CostEstimate(flops=0, bytes_accessed=0, transcendentals=0),
    )(*scalars, *arrays)


def exchange(keep, send):
    return keep + swap(send, 1)


def messages(total, shard):
    shards = total.shape[1]
    parts = [pick(total[0], shard)]
    for turn in range(shards):
        to = (shard + turn) % shards
        parts.append(hop(pick(total[1], to), 2, turn))
        if turn:
            parts.append(hop(pick(total[0], to), 0, turn))
    return parts


def after(value, *others):
    return lax.optimization_barrier((value, *others))[0]


def final_kernel(factor, counts, where_ref, *refs):
    out_ref, share_ref = refs[-2:]
    begin = 0
    for step, count in enumerate(counts):
        total = refs[begin][...]
        for ref in refs[begin + 1 : begin + count]:
            total = total + ref[...]
        share_ref[4 * step : 4 * step + 4] = total
        begin += count
    for d in range(out_ref.shape[0]):
        out_ref[d] = share_ref[where_ref[d]] * factor


def on_device(logder):
    nblocks = lax.axis_size("blk")
    nshards = lax.axis_size("par")
    rows, width = logder.shape
    me = lax.axis_index("blk")
    shard = lax.axis_index("par")
    planes = nblocks // 4
    steps = planes // 2
    tiles = nblocks // 2 + 1
    factor = 1.0 / (width * nshards)
    half, quarter, eighth = width // 2, width // 4, width // 8
    core, side = me & 1, (me >> 1) & 1
    plane = me // 4
    lead = plane // steps

    theirs = swap(lax.dynamic_slice_in_dim(logder, (1 - core) * half, half, 1), 1)
    sums = after(jnp.sum(logder, axis=0)[None], theirs)
    stride = 4
    while stride < nblocks:
        radix = min(4, nblocks // stride)
        moved = [swap(sums, k * stride) for k in range(1, radix)]
        sums = sum(moved, sums)
        stride *= radix

    def both(which, part):
        start = which * quarter + part * eighth
        mine = lax.dynamic_slice_in_dim(logder, core * half + start, eighth, 1)
        return jnp.stack([mine, lax.dynamic_slice_in_dim(theirs, start, eighth, 1)])

    near = both(side, lead), both(side, 1 - lead)
    far = swap(both(1 - side, lead), 2), swap(both(1 - side, 1 - lead), 2)
    first = [(near[0], far[0])]
    for step in range(steps):
        first.append(tuple(shift(value, -4) for value in first[-1]))
    second = [(after(near[1], *first[steps]), after(far[1], *first[steps]))]
    for step in range(steps - 1):
        second.append(tuple(shift(value, -4) for value in second[-1]))

    sums = after(sums, far[0])
    sums = lax.dynamic_slice_in_dim(sums, core * half, half, 1) + swap(
        lax.dynamic_slice_in_dim(sums, (1 - core) * half, half, 1), 1
    )
    sums = lax.dynamic_slice_in_dim(sums, side * quarter, quarter, 1) + swap(
        lax.dynamic_slice_in_dim(sums, (1 - side) * quarter, quarter, 1), 2
    )
    mean = after(sums, *first[steps]) / (rows * nblocks)
    mean = jnp.stack(
        [lax.dynamic_slice_in_dim(mean, part * eighth, eighth, 1) for part in (lead, 1 - lead)]
    )

    def tile_shape(count):
        return jax.ShapeDtypeStruct((2, nshards, count, rows // nshards, rows), jnp.float32)

    flops = 6 * 4 * rows * rows * quarter
    copies = jax.ShapeDtypeStruct((2, 2, 2 * rows, eighth), jnp.bfloat16)
    keep, send, high, low = call(
        own_kernel,
        (tile_shape(4), tile_shape(4), copies, copies),
        (),
        (near[0], far[0], near[1], far[1], mean),
        4 * flops,
    )
    own = keep, send

    keep, send = call(
        half_kernel,
        (tile_shape(8), tile_shape(8)),
        (),
        (mean, high, low, *first[steps]),
        4 * flops,
    )
    total = exchange(keep, send)
    last = messages(total, shard)
    shares = [messages(after(exchange(*own), total), shard)]
    pending = last

    mean = after(mean, total)
    for step in range(1, steps):
        flag = (((plane + step) % planes) // steps != lead).astype(jnp.int32)[None]
        keep, send = call(
            functools.partial(pair_kernel, (0,)),
            (tile_shape(4), tile_shape(4)),
            (flag,),
            (mean, high, low, first[step][0], second[step][0]),
            2 * flops,
        )
        keep, send = call(
            functools.partial(pair_kernel, (1,)),
            (tile_shape(4), tile_shape(4)),
            (flag,),
            (mean, high, low, first[step][1], second[step][1], keep, send),
            2 * flops,
        )
        total = exchange(keep, send)
        total = after(total, *pending)
        shares.append(messages(total, shard))
        pending = shares[-1]
    moved = sum(last[1:], last[0])
    tail = [moved[:4], shift(moved[4:], nblocks // 2)]
    shares.append(tail)

    place = me % 4
    position = place + jnp.arange(tiles, dtype=jnp.int32)
    where = position - position % 4 + ((position % 4) ^ place)
    counts = tuple(len(parts) for parts in shares)
    flat = [value for parts in shares for value in parts]
    out = pl.pallas_call(
        functools.partial(final_kernel, factor, counts),
        out_shape=jax.ShapeDtypeStruct((tiles, rows // nshards, rows), jnp.float32),
        in_specs=[SMEM] + [VMEM] * len(flat),
        out_specs=VMEM,
        scratch_shapes=[pltpu.VMEM((4 * (steps + 1), rows // nshards, rows), jnp.float32)],
    )(where, *flat)
    return out[None]


def solution(mesh):
    placed = (P("blk", "par"),)
    return jax.shard_map(
        on_device,
        mesh=mesh,
        in_specs=placed,
        out_specs=P("blk", None, "par", None),
        check_vma=False,
    )
```

```python
import functools
import jax
import jax.numpy as jnp
from jax import lax
from jax.experimental import pallas as pl
from jax.experimental.pallas import tpu as pltpu
from jax.sharding import PartitionSpec as P


def swap(value, mask):
    return lax.ppermute(value, "blk", [(k, k ^ mask) for k in range(lax.axis_size("blk"))])


def shift(value, steps):
    count = lax.axis_size("blk")
    return lax.ppermute(value, "blk", [(k, (k + steps) % count) for k in range(count)])


def hop(value, mask, turn):
    shards = lax.axis_size("par")
    pairs = [
        (k * shards + s, (k ^ mask) * shards + (s + turn) % shards)
        for k in range(lax.axis_size("blk"))
        for s in range(shards)
    ]
    return lax.ppermute(value, ("blk", "par"), pairs)


def pick(value, index, axis=0):
    return lax.dynamic_index_in_dim(value, index, axis, keepdims=False)


def split(value):
    high = value.astype(jnp.bfloat16)
    return high, (value - high.astype(jnp.float32)).astype(jnp.bfloat16)


def product(left, right):
    def dot(a, b):
        return lax.dot_general(
            a, b, (((1,), (1,)), ((), ())), preferred_element_type=jnp.float32
        )

    return dot(left[0], right[0]) + (dot(left[0], right[1]) + dot(left[1], right[0]))


def store(block, out_refs, a, b, first):
    keep_ref = out_refs[0]
    shards, part, rows = keep_ref.shape[1], keep_ref.shape[3], keep_ref.shape[4]
    for core, out in enumerate(out_refs):
        for other in range(2):
            place = first + ((2 * b + other) ^ (2 * a + core))
            tile = block[core * rows : (core + 1) * rows, other * rows : (other + 1) * rows]
            for s in range(shards):
                out[a, s, place] = tile[s * part : (s + 1) * part]


def centered(ref, mean):
    value = ref[...]
    return split(value.reshape(value.shape[0] * value.shape[1], value.shape[2]) - mean)


def own_kernel(near0, far0, near1, far1, mean_ref, keep_ref, send_ref, high_ref, low_ref):
    sides = []
    for chunk, refs in enumerate(((near0, far0), (near1, far1))):
        for a, ref in enumerate(refs):
            high, low = centered(ref, mean_ref[chunk])
            high_ref[chunk, a], low_ref[chunk, a] = high, low
            sides.append((high, low))
    for a in range(2):
        for b in range(2):
            block = product(sides[a], sides[b]) + product(sides[2 + a], sides[2 + b])
            store(block, (keep_ref, send_ref), a, b, 0)


def pair_kernel(columns, flag_ref, mean_ref, high_ref, low_ref, *refs):
    out_refs = refs[-2:]
    flag = flag_ref[0]
    if len(refs) > 2 * len(columns) + 2:
        for old, new in zip(refs[-4:-2], out_refs):
            for a in range(2):
                for place in range(4):
                    if (place ^ (2 * a)) // 2 not in columns:
                        new[a, :, place] = old[a, :, place]
    for position, b in enumerate(columns):
        rights = [
            centered(refs[2 * position + chunk], mean_ref[chunk ^ flag]) for chunk in range(2)
        ]
        for a in range(2):
            block = None
            for chunk in range(2):
                at = chunk ^ flag
                term = product((high_ref[at, a], low_ref[at, a]), rights[chunk])
                block = term if block is None else block + term
            store(block, out_refs, a, b, 0)


def half_kernel(mean_ref, high_ref, low_ref, near_ref, far_ref, keep_ref, send_ref):
    lefts = [(high_ref[1, a], low_ref[1, a]) for a in range(2)]
    rights = [centered(ref, mean_ref[1]) for ref in (near_ref, far_ref)]
    for a in range(2):
        for b in range(2):
            store(product(lefts[a], rights[b]), (keep_ref, send_ref), a, b, 0)
            store(product(rights[a], lefts[b]), (keep_ref, send_ref), a, b, 4)


VMEM = pl.BlockSpec(memory_space=pltpu.VMEM)
SMEM = pl.BlockSpec(memory_space=pltpu.SMEM)


def call(kernel, outs, scalars, arrays, flops):
    moved = sum(4 * v.size for v in arrays) + sum(4 * v.size for v in outs)
    return pl.pallas_call(
        kernel,
        out_shape=outs,
        in_specs=[SMEM] * len(scalars) + [VMEM] * len(arrays),
        out_specs=(VMEM,) * len(outs),
        compiler_params=pltpu.CompilerParams(vmem_limit_bytes=16 << 20),
        cost_estimate=pl.CostEstimate(flops=0, bytes_accessed=0, transcendentals=0),
    )(*scalars, *arrays)


def exchange(keep, send):
    return keep + swap(send, 1)


def messages(total, shard):
    shards = total.shape[1]
    parts = [pick(total[0], shard)]
    for turn in range(shards):
        to = (shard + turn) % shards
        parts.append(hop(pick(total[1], to), 2, turn))
        if turn:
            parts.append(hop(pick(total[0], to), 0, turn))
    return parts


def after(value, *others):
    return lax.optimization_barrier((value, *others))[0]


def final_kernel(factor, counts, where_ref, *refs):
    out_ref, share_ref = refs[-2:]
    begin = 0
    for step, count in enumerate(counts):
        total = refs[begin][...]
        for ref in refs[begin + 1 : begin + count]:
            total = total + ref[...]
        share_ref[4 * step : 4 * step + 4] = total
        begin += count
    for d in range(out_ref.shape[0]):
        out_ref[d] = share_ref[where_ref[d]] * factor


def on_device(logder):
    nblocks = lax.axis_size("blk")
    nshards = lax.axis_size("par")
    rows, width = logder.shape
    me = lax.axis_index("blk")
    shard = lax.axis_index("par")
    planes = nblocks // 4
    steps = planes // 2
    tiles = nblocks // 2 + 1
    factor = 1.0 / (width * nshards)
    half, quarter, eighth = width // 2, width // 4, width // 8
    core, side = me & 1, (me >> 1) & 1
    plane = me // 4
    lead = plane // steps

    theirs = swap(lax.dynamic_slice_in_dim(logder, (1 - core) * half, half, 1), 1)
    sums = jnp.sum(logder, axis=0)[None]
    stride = 4
    while stride < nblocks:
        radix = min(4, nblocks // stride)
        moved = [swap(sums, k * stride) for k in range(1, radix)]
        sums = sum(moved, sums)
        stride *= radix

    def both(which, part):
        start = which * quarter + part * eighth
        mine = lax.dynamic_slice_in_dim(logder, core * half + start, eighth, 1)
        return jnp.stack([mine, lax.dynamic_slice_in_dim(theirs, start, eighth, 1)])

    near = both(side, lead), both(side, 1 - lead)
    far = swap(both(1 - side, lead), 2), swap(both(1 - side, 1 - lead), 2)
    first = [(near[0], far[0])]
    for step in range(steps):
        first.append(tuple(shift(value, -4) for value in first[-1]))
    second = [(after(near[1], *first[steps]), after(far[1], *first[steps]))]
    for step in range(steps - 1):
        second.append(tuple(shift(value, -4) for value in second[-1]))

    sums = after(sums, far[0])
    sums = lax.dynamic_slice_in_dim(sums, core * half, half, 1) + swap(
        lax.dynamic_slice_in_dim(sums, (1 - core) * half, half, 1), 1
    )
    sums = lax.dynamic_slice_in_dim(sums, side * quarter, quarter, 1) + swap(
        lax.dynamic_slice_in_dim(sums, (1 - side) * quarter, quarter, 1), 2
    )
    mean = after(sums, *first[steps]) / (rows * nblocks)
    mean = jnp.stack(
        [lax.dynamic_slice_in_dim(mean, part * eighth, eighth, 1) for part in (lead, 1 - lead)]
    )

    def tile_shape(count):
        return jax.ShapeDtypeStruct((2, nshards, count, rows // nshards, rows), jnp.float32)

    flops = 6 * 4 * rows * rows * quarter
    copies = jax.ShapeDtypeStruct((2, 2, 2 * rows, eighth), jnp.bfloat16)
    keep, send, high, low = call(
        own_kernel,
        (tile_shape(4), tile_shape(4), copies, copies),
        (),
        (near[0], far[0], near[1], far[1], mean),
        4 * flops,
    )
    own = keep, send

    keep, send = call(
        half_kernel,
        (tile_shape(8), tile_shape(8)),
        (),
        (mean, high, low, *first[steps]),
        4 * flops,
    )
    total = exchange(keep, send)
    last = messages(total, shard)
    shares = [messages(exchange(after(own[0], total), own[1]), shard)]
    pending = last

    mean = after(mean, total)
    for step in range(1, steps):
        flag = (((plane + step) % planes) // steps != lead).astype(jnp.int32)[None]
        keep, send = call(
            functools.partial(pair_kernel, (0,)),
            (tile_shape(4), tile_shape(4)),
            (flag,),
            (mean, high, low, first[step][0], second[step][0]),
            2 * flops,
        )
        keep, send = call(
            functools.partial(pair_kernel, (1,)),
            (tile_shape(4), tile_shape(4)),
            (flag,),
            (mean, high, low, first[step][1], second[step][1], keep, send),
            2 * flops,
        )
        total = exchange(keep, send)
        total = after(total, *pending)
        shares.append(messages(total, shard))
        pending = shares[-1]
    moved = sum(last[1:], last[0])
    tail = [moved[:4], shift(moved[4:], nblocks // 2)]
    shares.append(tail)

    place = me % 4
    position = place + jnp.arange(tiles, dtype=jnp.int32)
    where = position - position % 4 + ((position % 4) ^ place)
    counts = tuple(len(parts) for parts in shares)
    flat = [value for parts in shares for value in parts]
    out = pl.pallas_call(
        functools.partial(final_kernel, factor, counts),
        out_shape=jax.ShapeDtypeStruct((tiles, rows // nshards, rows), jnp.float32),
        in_specs=[SMEM] + [VMEM] * len(flat),
        out_specs=VMEM,
        scratch_shapes=[pltpu.VMEM((4 * (steps + 1), rows // nshards, rows), jnp.float32)],
    )(where, *flat)
    return out[None]


def solution(mesh):
    placed = (P("blk", "par"),)
    return jax.shard_map(
        on_device,
        mesh=mesh,
        in_specs=placed,
        out_specs=P("blk", None, "par", None),
        check_vma=False,
    )
```

```python
import functools
import jax
import jax.numpy as jnp
from jax import lax
from jax.experimental import pallas as pl
from jax.experimental.pallas import tpu as pltpu
from jax.sharding import PartitionSpec as P


def swap(value, mask):
    return lax.ppermute(value, "blk", [(k, k ^ mask) for k in range(lax.axis_size("blk"))])


def shift(value, steps):
    count = lax.axis_size("blk")
    return lax.ppermute(value, "blk", [(k, (k + steps) % count) for k in range(count)])


def hop(value, mask, turn):
    shards = lax.axis_size("par")
    pairs = [
        (k * shards + s, (k ^ mask) * shards + (s + turn) % shards)
        for k in range(lax.axis_size("blk"))
        for s in range(shards)
    ]
    return lax.ppermute(value, ("blk", "par"), pairs)


def pick(value, index, axis=0):
    return lax.dynamic_index_in_dim(value, index, axis, keepdims=False)


def split(value):
    high = value.astype(jnp.bfloat16)
    return high, (value - high.astype(jnp.float32)).astype(jnp.bfloat16)


def product(left, right):
    def dot(a, b):
        return lax.dot_general(
            a, b, (((1,), (1,)), ((), ())), preferred_element_type=jnp.float32
        )

    return dot(left[0], right[0]) + (dot(left[0], right[1]) + dot(left[1], right[0]))


def store(block, out_refs, a, b, first):
    keep_ref = out_refs[0]
    shards, part, rows = keep_ref.shape[1], keep_ref.shape[3], keep_ref.shape[4]
    for core, out in enumerate(out_refs):
        for other in range(2):
            place = first + ((2 * b + other) ^ (2 * a + core))
            tile = block[core * rows : (core + 1) * rows, other * rows : (other + 1) * rows]
            for s in range(shards):
                out[a, s, place] = tile[s * part : (s + 1) * part]


def centered(ref, mean):
    value = ref[...]
    return split(value.reshape(value.shape[0] * value.shape[1], value.shape[2]) - mean)


def own_kernel(near0, far0, near1, far1, mean_ref, keep_ref, send_ref, high_ref, low_ref):
    sides = []
    for chunk, refs in enumerate(((near0, far0), (near1, far1))):
        for a, ref in enumerate(refs):
            high, low = centered(ref, mean_ref[chunk])
            high_ref[chunk, a], low_ref[chunk, a] = high, low
            sides.append((high, low))
    for a in range(2):
        for b in range(2):
            block = product(sides[a], sides[b]) + product(sides[2 + a], sides[2 + b])
            store(block, (keep_ref, send_ref), a, b, 0)


def pair_kernel(columns, flag_ref, mean_ref, high_ref, low_ref, *refs):
    out_refs = refs[-2:]
    flag = flag_ref[0]
    if len(refs) > 2 * len(columns) + 2:
        for old, new in zip(refs[-4:-2], out_refs):
            for a in range(2):
                for place in range(4):
                    if (place ^ (2 * a)) // 2 not in columns:
                        new[a, :, place] = old[a, :, place]
    for position, b in enumerate(columns):
        rights = [
            centered(refs[2 * position + chunk], mean_ref[chunk ^ flag]) for chunk in range(2)
        ]
        for a in range(2):
            block = None
            for chunk in range(2):
                at = chunk ^ flag
                term = product((high_ref[at, a], low_ref[at, a]), rights[chunk])
                block = term if block is None else block + term
            store(block, out_refs, a, b, 0)


def half_kernel(mean_ref, high_ref, low_ref, near_ref, far_ref, keep_ref, send_ref):
    lefts = [(high_ref[1, a], low_ref[1, a]) for a in range(2)]
    rights = [centered(ref, mean_ref[1]) for ref in (near_ref, far_ref)]
    for a in range(2):
        for b in range(2):
            store(product(lefts[a], rights[b]), (keep_ref, send_ref), a, b, 0)
            store(product(rights[a], lefts[b]), (keep_ref, send_ref), a, b, 4)


VMEM = pl.BlockSpec(memory_space=pltpu.VMEM)
SMEM = pl.BlockSpec(memory_space=pltpu.SMEM)


def call(kernel, outs, scalars, arrays, flops):
    moved = sum(4 * v.size for v in arrays) + sum(4 * v.size for v in outs)
    return pl.pallas_call(
        kernel,
        out_shape=outs,
        in_specs=[SMEM] * len(scalars) + [VMEM] * len(arrays),
        out_specs=(VMEM,) * len(outs),
        compiler_params=pltpu.CompilerParams(vmem_limit_bytes=16 << 20),
        cost_estimate=pl.CostEstimate(flops=0, bytes_accessed=0, transcendentals=0),
    )(*scalars, *arrays)


def exchange(keep, send):
    return keep + swap(send, 1)


def messages(total, shard):
    shards = total.shape[1]
    parts = [pick(total[0], shard)]
    for turn in range(shards):
        to = (shard + turn) % shards
        parts.append(hop(pick(total[1], to), 2, turn))
        if turn:
            parts.append(hop(pick(total[0], to), 0, turn))
    return parts


def after(value, *others):
    return lax.optimization_barrier((value, *others))[0]


def final_kernel(factor, counts, where_ref, *refs):
    out_ref, share_ref = refs[-2:]
    begin = 0
    for step, count in enumerate(counts):
        total = refs[begin][...]
        for ref in refs[begin + 1 : begin + count]:
            total = total + ref[...]
        share_ref[4 * step : 4 * step + 4] = total
        begin += count
    for d in range(out_ref.shape[0]):
        out_ref[d] = share_ref[where_ref[d]] * factor


def on_device(logder):
    nblocks = lax.axis_size("blk")
    nshards = lax.axis_size("par")
    rows, width = logder.shape
    me = lax.axis_index("blk")
    shard = lax.axis_index("par")
    planes = nblocks // 4
    steps = planes // 2
    tiles = nblocks // 2 + 1
    factor = 1.0 / (width * nshards)
    half, quarter, eighth = width // 2, width // 4, width // 8
    core, side = me & 1, (me >> 1) & 1
    plane = me // 4
    lead = plane // steps

    theirs = swap(lax.dynamic_slice_in_dim(logder, (1 - core) * half, half, 1), 1)
    sums = jnp.sum(logder, axis=0)[None]
    stride = 4
    while stride < nblocks:
        radix = min(4, nblocks // stride)
        moved = [swap(sums, k * stride) for k in range(1, radix)]
        sums = sum(moved, sums)
        stride *= radix

    def both(which, part):
        start = which * quarter + part * eighth
        mine = lax.dynamic_slice_in_dim(logder, core * half + start, eighth, 1)
        return jnp.stack([mine, lax.dynamic_slice_in_dim(theirs, start, eighth, 1)])

    near = both(side, lead), both(side, 1 - lead)
    far = swap(both(1 - side, lead), 2), swap(both(1 - side, 1 - lead), 2)
    first = [(near[0], far[0])]
    for step in range(steps):
        first.append(tuple(shift(value, -4) for value in first[-1]))
    second = [(after(near[1], *first[steps]), after(far[1], *first[steps]))]
    for step in range(steps - 1):
        second.append(tuple(shift(value, -4) for value in second[-1]))

    sums = after(sums, far[0])
    sums = lax.dynamic_slice_in_dim(sums, core * half, half, 1) + swap(
        lax.dynamic_slice_in_dim(sums, (1 - core) * half, half, 1), 1
    )
    sums = lax.dynamic_slice_in_dim(sums, side * quarter, quarter, 1) + swap(
        lax.dynamic_slice_in_dim(sums, (1 - side) * quarter, quarter, 1), 2
    )
    mean = after(sums, first[1][1]) / (rows * nblocks)
    mean = jnp.stack(
        [lax.dynamic_slice_in_dim(mean, part * eighth, eighth, 1) for part in (lead, 1 - lead)]
    )

    def tile_shape(count):
        return jax.ShapeDtypeStruct((2, nshards, count, rows // nshards, rows), jnp.float32)

    flops = 6 * 4 * rows * rows * quarter
    copies = jax.ShapeDtypeStruct((2, 2, 2 * rows, eighth), jnp.bfloat16)
    keep, send, high, low = call(
        own_kernel,
        (tile_shape(4), tile_shape(4), copies, copies),
        (),
        (near[0], far[0], near[1], far[1], mean),
        4 * flops,
    )
    own = keep, send

    keep, send = call(
        half_kernel,
        (tile_shape(8), tile_shape(8)),
        (),
        (mean, high, low, *first[steps]),
        4 * flops,
    )
    first_total = exchange(*own)
    shares = [messages(first_total, shard)]
    total = after(exchange(keep, send), first_total)
    last = messages(total, shard)
    pending = last

    mean = after(mean, total)
    for step in range(1, steps):
        flag = (((plane + step) % planes) // steps != lead).astype(jnp.int32)[None]
        keep, send = call(
            functools.partial(pair_kernel, (0,)),
            (tile_shape(4), tile_shape(4)),
            (flag,),
            (mean, high, low, first[step][0], second[step][0]),
            2 * flops,
        )
        keep, send = call(
            functools.partial(pair_kernel, (1,)),
            (tile_shape(4), tile_shape(4)),
            (flag,),
            (mean, high, low, first[step][1], second[step][1], keep, send),
            2 * flops,
        )
        total = exchange(keep, send)
        total = after(total, *pending)
        shares.append(messages(total, shard))
        pending = shares[-1]
    moved = sum(last[1:], last[0])
    tail = [moved[:4], shift(moved[4:], nblocks // 2)]
    shares.append(tail)

    place = me % 4
    position = place + jnp.arange(tiles, dtype=jnp.int32)
    where = position - position % 4 + ((position % 4) ^ place)
    counts = tuple(len(parts) for parts in shares)
    flat = [value for parts in shares for value in parts]
    out = pl.pallas_call(
        functools.partial(final_kernel, factor, counts),
        out_shape=jax.ShapeDtypeStruct((tiles, rows // nshards, rows), jnp.float32),
        in_specs=[SMEM] + [VMEM] * len(flat),
        out_specs=VMEM,
        scratch_shapes=[pltpu.VMEM((4 * (steps + 1), rows // nshards, rows), jnp.float32)],
    )(where, *flat)
    return out[None]


def solution(mesh):
    placed = (P("blk", "par"),)
    return jax.shard_map(
        on_device,
        mesh=mesh,
        in_specs=placed,
        out_specs=P("blk", None, "par", None),
        check_vma=False,
    )
```

```python
import functools
import jax
import jax.numpy as jnp
from jax import lax
from jax.experimental import pallas as pl
from jax.experimental.pallas import tpu as pltpu
from jax.sharding import PartitionSpec as P


def swap(value, mask):
    return lax.ppermute(value, "blk", [(k, k ^ mask) for k in range(lax.axis_size("blk"))])


def shift(value, steps):
    count = lax.axis_size("blk")
    return lax.ppermute(value, "blk", [(k, (k + steps) % count) for k in range(count)])


def hop(value, mask, turn):
    shards = lax.axis_size("par")
    pairs = [
        (k * shards + s, (k ^ mask) * shards + (s + turn) % shards)
        for k in range(lax.axis_size("blk"))
        for s in range(shards)
    ]
    return lax.ppermute(value, ("blk", "par"), pairs)


def pick(value, index, axis=0):
    return lax.dynamic_index_in_dim(value, index, axis, keepdims=False)


def split(value):
    high = value.astype(jnp.bfloat16)
    return high, (value - high.astype(jnp.float32)).astype(jnp.bfloat16)


def product(left, right):
    def dot(a, b):
        return lax.dot_general(
            a, b, (((1,), (1,)), ((), ())), preferred_element_type=jnp.float32
        )

    return dot(left[0], right[0]) + (dot(left[0], right[1]) + dot(left[1], right[0]))


def store(block, out_refs, a, b, first):
    keep_ref = out_refs[0]
    shards, part, rows = keep_ref.shape[1], keep_ref.shape[3], keep_ref.shape[4]
    for core, out in enumerate(out_refs):
        for other in range(2):
            place = first + ((2 * b + other) ^ (2 * a + core))
            tile = block[core * rows : (core + 1) * rows, other * rows : (other + 1) * rows]
            for s in range(shards):
                out[a, s, place] = tile[s * part : (s + 1) * part]


def centered(ref, mean):
    value = ref[...]
    return split(value.reshape(value.shape[0] * value.shape[1], value.shape[2]) - mean)


def own_kernel(near0, far0, near1, far1, mean_ref, keep_ref, send_ref, high_ref, low_ref):
    sides = []
    for chunk, refs in enumerate(((near0, far0), (near1, far1))):
        for a, ref in enumerate(refs):
            high, low = centered(ref, mean_ref[chunk])
            high_ref[chunk, a], low_ref[chunk, a] = high, low
            sides.append((high, low))
    for a in range(2):
        for b in range(2):
            block = product(sides[a], sides[b]) + product(sides[2 + a], sides[2 + b])
            store(block, (keep_ref, send_ref), a, b, 0)


def pair_kernel(columns, flag_ref, mean_ref, high_ref, low_ref, *refs):
    out_refs = refs[-2:]
    flag = flag_ref[0]
    if len(refs) > 2 * len(columns) + 2:
        for old, new in zip(refs[-4:-2], out_refs):
            for a in range(2):
                for place in range(4):
                    if (place ^ (2 * a)) // 2 not in columns:
                        new[a, :, place] = old[a, :, place]
    for position, b in enumerate(columns):
        rights = [
            centered(refs[2 * position + chunk], mean_ref[chunk ^ flag]) for chunk in range(2)
        ]
        for a in range(2):
            block = None
            for chunk in range(2):
                at = chunk ^ flag
                term = product((high_ref[at, a], low_ref[at, a]), rights[chunk])
                block = term if block is None else block + term
            store(block, out_refs, a, b, 0)


def half_kernel(column, mean_ref, high_ref, low_ref, right_ref, *refs):
    out_refs = refs[-2:]
    for old, new in zip(refs[:-2], out_refs):
        new[1 - column, :, 4:] = old[1 - column, :, 4:]
        for a in range(2):
            for place in range(4):
                if (place ^ (2 * a)) // 2 != column:
                    new[a, :, place] = old[a, :, place]
    lefts = [(high_ref[1, a], low_ref[1, a]) for a in range(2)]
    right = centered(right_ref, mean_ref[1])
    for a in range(2):
        store(product(lefts[a], right), out_refs, a, column, 0)
        store(product(right, lefts[a]), out_refs, column, a, 4)


VMEM = pl.BlockSpec(memory_space=pltpu.VMEM)
SMEM = pl.BlockSpec(memory_space=pltpu.SMEM)


def call(kernel, outs, scalars, arrays, flops):
    moved = sum(4 * v.size for v in arrays) + sum(4 * v.size for v in outs)
    return pl.pallas_call(
        kernel,
        out_shape=outs,
        in_specs=[SMEM] * len(scalars) + [VMEM] * len(arrays),
        out_specs=(VMEM,) * len(outs),
        compiler_params=pltpu.CompilerParams(vmem_limit_bytes=16 << 20),
        cost_estimate=pl.CostEstimate(flops=0, bytes_accessed=0, transcendentals=0),
    )(*scalars, *arrays)


def exchange(keep, send):
    return keep + swap(send, 1)


def messages(total, shard):
    shards = total.shape[1]
    parts = [pick(total[0], shard)]
    for turn in range(shards):
        to = (shard + turn) % shards
        parts.append(hop(pick(total[1], to), 2, turn))
        if turn:
            parts.append(hop(pick(total[0], to), 0, turn))
    return parts


def after(value, *others):
    return lax.optimization_barrier((value, *others))[0]


def final_kernel(factor, counts, where_ref, *refs):
    out_ref, share_ref = refs[-2:]
    begin = 0
    for step, count in enumerate(counts):
        total = refs[begin][...]
        for ref in refs[begin + 1 : begin + count]:
            total = total + ref[...]
        share_ref[4 * step : 4 * step + 4] = total
        begin += count
    for d in range(out_ref.shape[0]):
        out_ref[d] = share_ref[where_ref[d]] * factor


def on_device(logder):
    nblocks = lax.axis_size("blk")
    nshards = lax.axis_size("par")
    rows, width = logder.shape
    me = lax.axis_index("blk")
    shard = lax.axis_index("par")
    planes = nblocks // 4
    steps = planes // 2
    tiles = nblocks // 2 + 1
    factor = 1.0 / (width * nshards)
    half, quarter, eighth = width // 2, width // 4, width // 8
    core, side = me & 1, (me >> 1) & 1
    plane = me // 4
    lead = plane // steps

    theirs = swap(lax.dynamic_slice_in_dim(logder, (1 - core) * half, half, 1), 1)
    sums = jnp.sum(logder, axis=0)[None]
    stride = 4
    while stride < nblocks:
        radix = min(4, nblocks // stride)
        moved = [swap(sums, k * stride) for k in range(1, radix)]
        sums = sum(moved, sums)
        stride *= radix

    def both(which, part):
        start = which * quarter + part * eighth
        mine = lax.dynamic_slice_in_dim(logder, core * half + start, eighth, 1)
        return jnp.stack([mine, lax.dynamic_slice_in_dim(theirs, start, eighth, 1)])

    near = both(side, lead), both(side, 1 - lead)
    far = swap(both(1 - side, lead), 2), swap(both(1 - side, 1 - lead), 2)
    first = [(near[0], far[0])]
    for step in range(steps):
        first.append(tuple(shift(value, -4) for value in first[-1]))
    second = [(after(near[1], *first[steps]), after(far[1], *first[steps]))]
    for step in range(steps - 1):
        second.append(tuple(shift(value, -4) for value in second[-1]))

    sums = after(sums, far[0])
    sums = lax.dynamic_slice_in_dim(sums, core * half, half, 1) + swap(
        lax.dynamic_slice_in_dim(sums, (1 - core) * half, half, 1), 1
    )
    sums = lax.dynamic_slice_in_dim(sums, side * quarter, quarter, 1) + swap(
        lax.dynamic_slice_in_dim(sums, (1 - side) * quarter, quarter, 1), 2
    )
    mean = after(sums, first[1][1]) / (rows * nblocks)
    mean = jnp.stack(
        [lax.dynamic_slice_in_dim(mean, part * eighth, eighth, 1) for part in (lead, 1 - lead)]
    )

    def tile_shape(count):
        return jax.ShapeDtypeStruct((2, nshards, count, rows // nshards, rows), jnp.float32)

    flops = 6 * 4 * rows * rows * quarter
    copies = jax.ShapeDtypeStruct((2, 2, 2 * rows, eighth), jnp.bfloat16)
    keep, send, high, low = call(
        own_kernel,
        (tile_shape(4), tile_shape(4), copies, copies),
        (),
        (near[0], far[0], near[1], far[1], mean),
        4 * flops,
    )
    own = keep, send

    outs = ()
    for column in range(2):
        outs = call(
            functools.partial(half_kernel, column),
            (tile_shape(8), tile_shape(8)),
            (),
            (mean, high, low, first[steps][column], *outs),
            2 * flops,
        )
    keep, send = outs
    first_total = exchange(*own)
    shares = [messages(first_total, shard)]
    total = after(exchange(keep, send), first_total)
    last = messages(total, shard)
    pending = last

    mean = after(mean, total)
    for step in range(1, steps):
        flag = (((plane + step) % planes) // steps != lead).astype(jnp.int32)[None]
        keep, send = call(
            functools.partial(pair_kernel, (0,)),
            (tile_shape(4), tile_shape(4)),
            (flag,),
            (mean, high, low, first[step][0], second[step][0]),
            2 * flops,
        )
        keep, send = call(
            functools.partial(pair_kernel, (1,)),
            (tile_shape(4), tile_shape(4)),
            (flag,),
            (mean, high, low, first[step][1], second[step][1], keep, send),
            2 * flops,
        )
        total = exchange(keep, send)
        total = after(total, *pending)
        shares.append(messages(total, shard))
        pending = shares[-1]
    moved = sum(last[1:], last[0])
    tail = [moved[:4], shift(moved[4:], nblocks // 2)]
    shares.append(tail)

    place = me % 4
    position = place + jnp.arange(tiles, dtype=jnp.int32)
    where = position - position % 4 + ((position % 4) ^ place)
    counts = tuple(len(parts) for parts in shares)
    flat = [value for parts in shares for value in parts]
    out = pl.pallas_call(
        functools.partial(final_kernel, factor, counts),
        out_shape=jax.ShapeDtypeStruct((tiles, rows // nshards, rows), jnp.float32),
        in_specs=[SMEM] + [VMEM] * len(flat),
        out_specs=VMEM,
        scratch_shapes=[pltpu.VMEM((4 * (steps + 1), rows // nshards, rows), jnp.float32)],
    )(where, *flat)
    return out[None]


def solution(mesh):
    placed = (P("blk", "par"),)
    return jax.shard_map(
        on_device,
        mesh=mesh,
        in_specs=placed,
        out_specs=P("blk", None, "par", None),
        check_vma=False,
    )
```

```python
import functools
import jax
import jax.numpy as jnp
from jax import lax
from jax.experimental import pallas as pl
from jax.experimental.pallas import tpu as pltpu
from jax.sharding import PartitionSpec as P


def swap(value, mask):
    return lax.ppermute(value, "blk", [(k, k ^ mask) for k in range(lax.axis_size("blk"))])


def shift(value, steps):
    count = lax.axis_size("blk")
    return lax.ppermute(value, "blk", [(k, (k + steps) % count) for k in range(count)])


def hop(value, mask, turn):
    shards = lax.axis_size("par")
    pairs = [
        (k * shards + s, (k ^ mask) * shards + (s + turn) % shards)
        for k in range(lax.axis_size("blk"))
        for s in range(shards)
    ]
    return lax.ppermute(value, ("blk", "par"), pairs)


def pick(value, index, axis=0):
    return lax.dynamic_index_in_dim(value, index, axis, keepdims=False)


def split(value):
    high = value.astype(jnp.bfloat16)
    return high, (value - high.astype(jnp.float32)).astype(jnp.bfloat16)


def product(left, right):
    def dot(a, b):
        return lax.dot_general(
            a, b, (((1,), (1,)), ((), ())), preferred_element_type=jnp.float32
        )

    return dot(left[0], right[0]) + (dot(left[0], right[1]) + dot(left[1], right[0]))


def store(block, out_refs, a, b, first):
    keep_ref = out_refs[0]
    shards, part, rows = keep_ref.shape[1], keep_ref.shape[3], keep_ref.shape[4]
    for core, out in enumerate(out_refs):
        for other in range(2):
            place = first + ((2 * b + other) ^ (2 * a + core))
            tile = block[core * rows : (core + 1) * rows, other * rows : (other + 1) * rows]
            for s in range(shards):
                out[a, s, place] = tile[s * part : (s + 1) * part]


def centered(ref, mean):
    value = ref[...]
    return split(value.reshape(value.shape[0] * value.shape[1], value.shape[2]) - mean)


def own_kernel(near0, far0, near1, far1, mean_ref, keep_ref, send_ref, high_ref, low_ref):
    sides = []
    for chunk, refs in enumerate(((near0, far0), (near1, far1))):
        for a, ref in enumerate(refs):
            high, low = centered(ref, mean_ref[chunk])
            high_ref[chunk, a], low_ref[chunk, a] = high, low
            sides.append((high, low))
    for a in range(2):
        for b in range(2):
            block = product(sides[a], sides[b]) + product(sides[2 + a], sides[2 + b])
            store(block, (keep_ref, send_ref), a, b, 0)


def pair_kernel(columns, flag_ref, mean_ref, high_ref, low_ref, *refs):
    out_refs = refs[-2:]
    flag = flag_ref[0]
    if len(refs) > 2 * len(columns) + 2:
        for old, new in zip(refs[-4:-2], out_refs):
            for a in range(2):
                for place in range(4):
                    if (place ^ (2 * a)) // 2 not in columns:
                        new[a, :, place] = old[a, :, place]
    for position, b in enumerate(columns):
        rights = [
            centered(refs[2 * position + chunk], mean_ref[chunk ^ flag]) for chunk in range(2)
        ]
        for a in range(2):
            block = None
            for chunk in range(2):
                at = chunk ^ flag
                term = product((high_ref[at, a], low_ref[at, a]), rights[chunk])
                block = term if block is None else block + term
            store(block, out_refs, a, b, 0)


def half_kernel(column, mean_ref, high_ref, low_ref, right_ref, *refs):
    out_refs = refs[-2:]
    for old, new in zip(refs[:-2], out_refs):
        new[1 - column, :, 4:] = old[1 - column, :, 4:]
        for a in range(2):
            for place in range(4):
                if (place ^ (2 * a)) // 2 != column:
                    new[a, :, place] = old[a, :, place]
    lefts = [(high_ref[1, a], low_ref[1, a]) for a in range(2)]
    right = centered(right_ref, mean_ref[1])
    for a in range(2):
        store(product(lefts[a], right), out_refs, a, column, 0)
        store(product(right, lefts[a]), out_refs, column, a, 4)


VMEM = pl.BlockSpec(memory_space=pltpu.VMEM)
SMEM = pl.BlockSpec(memory_space=pltpu.SMEM)


def call(kernel, outs, scalars, arrays, flops):
    moved = sum(4 * v.size for v in arrays) + sum(4 * v.size for v in outs)
    return pl.pallas_call(
        kernel,
        out_shape=outs,
        in_specs=[SMEM] * len(scalars) + [VMEM] * len(arrays),
        out_specs=(VMEM,) * len(outs),
        compiler_params=pltpu.CompilerParams(vmem_limit_bytes=16 << 20),
        cost_estimate=pl.CostEstimate(flops=0, bytes_accessed=0, transcendentals=0),
    )(*scalars, *arrays)


def exchange(keep, send):
    return keep + swap(send, 1)


def messages(total, shard):
    shards = total.shape[1]
    parts = [pick(total[0], shard)]
    for turn in range(shards):
        to = (shard + turn) % shards
        parts.append(hop(pick(total[1], to), 2, turn))
        if turn:
            parts.append(hop(pick(total[0], to), 0, turn))
    return parts


def after(value, *others):
    return lax.optimization_barrier((value, *others))[0]


def final_kernel(factor, counts, where_ref, *refs):
    out_ref, share_ref = refs[-2:]
    begin = 0
    for step, count in enumerate(counts):
        total = refs[begin][...]
        for ref in refs[begin + 1 : begin + count]:
            total = total + ref[...]
        share_ref[4 * step : 4 * step + 4] = total
        begin += count
    for d in range(out_ref.shape[0]):
        out_ref[d] = share_ref[where_ref[d]] * factor


def on_device(logder):
    nblocks = lax.axis_size("blk")
    nshards = lax.axis_size("par")
    rows, width = logder.shape
    me = lax.axis_index("blk")
    shard = lax.axis_index("par")
    planes = nblocks // 4
    steps = planes // 2
    tiles = nblocks // 2 + 1
    factor = 1.0 / (width * nshards)
    half, quarter, eighth = width // 2, width // 4, width // 8
    core, side = me & 1, (me >> 1) & 1
    plane = me // 4
    lead = plane // steps

    theirs = swap(lax.dynamic_slice_in_dim(logder, (1 - core) * half, half, 1), 1)
    sums = jnp.sum(logder, axis=0)[None]
    stride = 4
    while stride < nblocks:
        radix = min(4, nblocks // stride)
        moved = [swap(sums, k * stride) for k in range(1, radix)]
        sums = sum(moved, sums)
        stride *= radix

    def both(which, part):
        start = which * quarter + part * eighth
        mine = lax.dynamic_slice_in_dim(logder, core * half + start, eighth, 1)
        return jnp.stack([mine, lax.dynamic_slice_in_dim(theirs, start, eighth, 1)])

    near = both(side, lead), both(side, 1 - lead)
    far = swap(both(1 - side, lead), 2), swap(both(1 - side, 1 - lead), 2)
    first = [(near[0], far[0])]
    for step in range(steps):
        first.append(tuple(shift(value, -4) for value in first[-1]))
    second = [(after(near[1], *first[steps]), after(far[1], *first[steps]))]
    for step in range(steps - 1):
        second.append(tuple(shift(value, -4) for value in second[-1]))

    sums = after(sums, far[0])
    sums = lax.dynamic_slice_in_dim(sums, core * half, half, 1) + swap(
        lax.dynamic_slice_in_dim(sums, (1 - core) * half, half, 1), 1
    )
    sums = lax.dynamic_slice_in_dim(sums, side * quarter, quarter, 1) + swap(
        lax.dynamic_slice_in_dim(sums, (1 - side) * quarter, quarter, 1), 2
    )
    mean = after(sums, first[1][1]) / (rows * nblocks)
    mean = jnp.stack(
        [lax.dynamic_slice_in_dim(mean, part * eighth, eighth, 1) for part in (lead, 1 - lead)]
    )

    def tile_shape(count):
        return jax.ShapeDtypeStruct((2, nshards, count, rows // nshards, rows), jnp.float32)

    flops = 6 * 4 * rows * rows * quarter
    copies = jax.ShapeDtypeStruct((2, 2, 2 * rows, eighth), jnp.bfloat16)
    keep, send, high, low = call(
        own_kernel,
        (tile_shape(4), tile_shape(4), copies, copies),
        (),
        (near[0], far[0], near[1], far[1], mean),
        4 * flops,
    )
    own = keep, send

    outs = ()
    for column in range(2):
        outs = call(
            functools.partial(half_kernel, column),
            (tile_shape(8), tile_shape(8)),
            (),
            (mean, high, low, first[steps][column], *outs),
            2 * flops,
        )
    keep, send = outs
    total = exchange(keep, send)
    last = messages(total, shard)
    shares = [messages(after(exchange(*own), total), shard)]
    pending = last

    mean = after(mean, total)
    for step in range(1, steps):
        flag = (((plane + step) % planes) // steps != lead).astype(jnp.int32)[None]
        keep, send = call(
            functools.partial(pair_kernel, (0,)),
            (tile_shape(4), tile_shape(4)),
            (flag,),
            (mean, high, low, first[step][0], second[step][0]),
            2 * flops,
        )
        keep, send = call(
            functools.partial(pair_kernel, (1,)),
            (tile_shape(4), tile_shape(4)),
            (flag,),
            (mean, high, low, first[step][1], second[step][1], keep, send),
            2 * flops,
        )
        total = exchange(keep, send)
        total = after(total, *pending)
        shares.append(messages(total, shard))
        pending = shares[-1]
    moved = sum(last[1:], last[0])
    tail = [moved[:4], shift(moved[4:], nblocks // 2)]
    shares.append(tail)

    place = me % 4
    position = place + jnp.arange(tiles, dtype=jnp.int32)
    where = position - position % 4 + ((position % 4) ^ place)
    counts = tuple(len(parts) for parts in shares)
    flat = [value for parts in shares for value in parts]
    out = pl.pallas_call(
        functools.partial(final_kernel, factor, counts),
        out_shape=jax.ShapeDtypeStruct((tiles, rows // nshards, rows), jnp.float32),
        in_specs=[SMEM] + [VMEM] * len(flat),
        out_specs=VMEM,
        scratch_shapes=[pltpu.VMEM((4 * (steps + 1), rows // nshards, rows), jnp.float32)],
    )(where, *flat)
    return out[None]


def solution(mesh):
    placed = (P("blk", "par"),)
    return jax.shard_map(
        on_device,
        mesh=mesh,
        in_specs=placed,
        out_specs=P("blk", None, "par", None),
        check_vma=False,
    )
```
